32 devices in a mesh: grp: 4 (over z), pen: 8 (over y, x, core).
Axes of the slice: x: 2, y: 2, z: 4, core: 2. Of those that a mesh axis runs over, the one named last changes fastest.
Arguments:
- psi: float32 [2, 512, 128, 512], P(None, 'pen', 'grp'), may hold values from -6 to 6
- potential: float32 [512, 128, 512], P('pen', 'grp'), may hold values from -20 to 20
- absorber_region: int32 [512, 128], P('pen', 'grp'), may hold values from 0 to 3
- absorber_strength: float32 [4], replicated, may hold values from 0.5 to 8
- route_owner: int32 [4, 8, 2048, 2], P('grp', 'pen'), may hold values from 0 to 7, all different within a row; in each aligned block of 2048 rows (0 to 2047, 2048 to 4095, ..., all dimensions but the last counted through in order) at most 1024 rows name the same one
- route_row: int32 [4, 8, 2048, 2], P('grp', 'pen'), may hold values from 0 to 63
- route_weight: float32 [4, 8, 2048, 2], P('grp', 'pen'), may hold values from 0.25 to 1
Outputs:
- psi_final: float32 [2, 512, 128, 512], P(None, 'pen', 'grp')
- product_flux: float32 [4, 8, 64, 256], P('grp', 'pen')
The draws below stay inside these ranges and needn't reach their ends.
Inputs may be any that keep to these rules, and one draw needn't show every extreme that they name: `route_owner`: in each device's 2048 rows (aligned blocks of 2048 rows) no owner is named by more than 1024 rows, a bound that some block reaches; the two owners of a row differ.
All inputs are finite; a program needn't handle non-finite values.
Results may differ from the reference program's by a relative error of at most 0.029.
Values may be sent and summed in bfloat16 or wider, within the bound.
A program may use at most 128 MiB of HBM per device.

```python
import math
import jax
import jax.numpy as jnp
import numpy as np
from jax import lax

NS = 512
NL = 512
NANG = 128
RABS = 128
STEPS = 2
NREGION = 4
PSROWS = 64
R_DEV = 64
A_DEV = 32
BLK = 2048
CAP = 1024
N_GRP = 4
N_PEN = 8


def place_ends(drawn, rng, least, top_value):
    index_at = [jax.random.randint(jax.random.fold_in(rng, axis), (), 0, length) for axis, length in enumerate(drawn.shape)]
    longest = drawn.shape.index(max(drawn.shape))
    neighbour = index_at[:longest] + [(index_at[longest] + 1) % drawn.shape[longest]] + index_at[longest + 1:]
    return drawn.at[tuple(index_at)].set(least).at[tuple(neighbour)].set(top_value)


def level_of(key, dims, cuts, least, high):
    loudness, own = 1.0, jax.random.fold_in(key, 6)
    for dim, blocks in cuts:
        heights = jnp.exp(jax.random.uniform(jax.random.fold_in(own, dim), (blocks,), jnp.float32, least / len(cuts), high / len(cuts)))
        loudness = loudness * jnp.repeat(heights, dims[dim] // blocks).reshape([-1 if axis == dim else 1 for axis in range(len(dims))])
    return loudness


def assign_block(own_key, own, number, rows, amount, top, limit, skew):
    ranking = jax.random.permutation(own_key, amount)
    heavy_load, ordinary = shares(amount, rows * top, limit, skew, True), shares(amount, rows * top, limit, skew, False)
    places = jnp.arange(amount)

    def named(tallies, rotation):
        used = int((tallies > 0).sum())
        fixed = max(1, used // 4)
        shifted = fixed + (places - fixed + rotation * (used - fixed)) % max(1, amount - fixed)
        return jnp.zeros((amount,), jnp.int32).at[ranking[jnp.where(places < fixed, places, shifted)]].set(jnp.asarray(tallies, jnp.int32))

    tallies = jnp.where(number % 4 == 0, named(heavy_load, number // 4), named(ordinary, number - number // 4 - 1))
    mixed = jax.random.permutation(jax.random.fold_in(own, 3), amount)
    source_of, sink = mixed[0:amount // 2 * 2:2], mixed[1:amount // 2 * 2:2]
    slack = jnp.minimum(tallies[source_of] - 1, limit - tallies[sink]) // 2
    slack = jnp.where((source_of == ranking[0]) | (sink == ranking[0]) | (tallies[sink] == 0), 0, jnp.maximum(slack, 0))
    shifted = jax.random.randint(jax.random.fold_in(own, 4), (amount // 2,), 0, 1 << 20) % (slack + 1)
    tallies = tallies.at[source_of].add(-shifted).at[sink].add(shifted)
    members = jnp.searchsorted(jnp.cumsum(tallies), jnp.arange(rows * top), side="right").astype(jnp.int32)
    listing = members.reshape(top, rows).T
    listing = listing[jax.random.permutation(jax.random.fold_in(own, 1), rows)]
    rotation = jax.random.randint(jax.random.fold_in(own, 2), (rows, 1), 0, top)
    return jnp.take_along_axis(listing, (jnp.arange(top)[None, :] + rotation) % top, axis=1)


def shares(count, total, most, skew, full):
    weights = [(1 << 20) // math.isqrt(grade ** skew) + 1 for grade in range(1, count + 1)]
    largest = most if full else min(most, max(-(-total // count), total * weights[0] // sum(weights)))
    least = 1 if total - largest >= count - 1 else 0
    given, spare = [largest] + [least] * (count - 1), total - largest - least * (count - 1)
    while spare > 0:
        free = [i for i in range(1, count) if given[i] < largest] or [i for i in range(1, count) if given[i] < most]
        mass, budget = sum([weights[i] for i in free]), spare
        for i in free:
            addition = min(most - given[i], max(1, budget * weights[i] // mass), spare)
            given[i] = given[i] + addition
            spare = spare - addition
    return np.array(given)


def gaussian(key, dims, width, most, shards=(), kind=jnp.bfloat16):
    array = jax.random.normal(key, dims, jnp.float32) * width
    if len(shards) > 0:
        array = level_of(key, dims, shards, -0.22, 0.18) * array
    return jnp.clip(array, min=-most, max=most).astype(kind)


def setup_inputs(seed: int = 0) -> dict:
    seeds = jax.random.split(jax.random.key(seed), 8)
    psi = gaussian(seeds[0], (2, NL, NANG, NS), 1.0, 6.0, ((1, 8), (2, 4)), jnp.float32)
    potential = jnp.clip(jax.random.uniform(seeds[1], (NL, NANG, NS), jnp.float32, -20.0, 20.0) * level_of(seeds[1], (NL, NANG, NS), ((0, 8), (1, 4)), -0.4, 0.0), -20.0, 20.0)
    absorber_region = place_ends(jax.random.randint(seeds[2], (NL, NANG), 0, NREGION), jax.random.fold_in(seeds[2], 1), 0, NREGION - 1).astype(jnp.int32)
    absorber_strength = jnp.clip(jnp.exp(jax.random.uniform(seeds[3], (NREGION,), jnp.float32, math.log(0.5), math.log(8.0))), 0.5, 8.0)
    route_owner_keys = jax.random.split(jax.random.fold_in(seeds[4], 1), N_GRP * N_PEN * BLK // BLK)
    route_owner_turns = jax.random.permutation(jax.random.fold_in(seeds[4], 3), N_GRP * N_PEN * BLK // BLK)
    route_owner = jax.vmap(lambda own, number: assign_block(jax.random.fold_in(seeds[4], 2), own, number, BLK, N_PEN, 2, CAP, 2))(route_owner_keys, route_owner_turns).reshape((N_GRP, N_PEN, BLK, 2))
    route_row = place_ends(jax.random.randint(seeds[5], (N_GRP, N_PEN, BLK, 2), 0, PSROWS), jax.random.fold_in(seeds[5], 1), 0, PSROWS - 1).astype(jnp.int32)
    route_weight = jnp.clip(0.25 + 0.75 * jax.random.uniform(seeds[6], (N_GRP, N_PEN, BLK, 2), jnp.float32) ** level_of(seeds[6], (N_GRP, N_PEN, BLK, 2), ((0, 4), (1, 8)), -0.2, 0.2), 0.25, 1.0)
    return dict(psi=psi, potential=potential, absorber_region=absorber_region, absorber_strength=absorber_strength, route_owner=route_owner, route_row=route_row, route_weight=route_weight)


time_step = 0.05
grid_spacing = 0.1
reduced_mass = 0.999456
energy_cap = 500.0

def sine_table(count):
    counter = jnp.arange(count, dtype=jnp.int32) + 1
    product = counter[:, None] * counter[None, :] % (2 * (count + 1))
    angles = jnp.pi * product.astype(jnp.float32) / (count + 1)
    return (math.sqrt(2.0 / (count + 1)) * jnp.sin(angles)).astype(jnp.bfloat16)

def kinetic_phase(count):
    wave = jnp.pi * (jnp.arange(count, dtype=jnp.float32) + 1.0) / (grid_spacing * (count + 1))
    angle_now = time_step * wave * wave / (2.0 * reduced_mass)
    return (jnp.cos(angle_now), jnp.sin(angle_now))

def rotate(real_part, imag_part, cosine, sine_part):
    return (real_part * cosine + imag_part * sine_part, imag_part * cosine - real_part * sine_part)

def legendre_pair(points, count):

    def advance_degree(degree_index, carry):
        previous, current = carry
        degree = degree_index.astype(points.dtype)
        following = ((2.0 * degree + 1.0) * points * current - degree * previous) / (degree + 1.0)
        return (current, following)
    return lax.fori_loop(1, count, advance_degree, (jnp.ones_like(points), points))

def legendre_table(count):
    counter = jnp.arange(count, dtype=jnp.float32)
    points = jnp.cos(jnp.pi * (counter + 0.75) / (count + 0.5))
    for newton_round in range(8):
        previous, current = legendre_pair(points, count)
        slope = count * (points * current - previous) / (points * points - 1.0)
        points = points - current / slope
    previous, current = legendre_pair(points, count)
    slope = count * (points * current - previous) / (points * points - 1.0)
    weights = 2.0 / ((1.0 - points * points) * slope * slope)

    def emit_row(carry, degree_index):
        lower, upper = carry
        degree = degree_index.astype(points.dtype) + 1.0
        following = ((2.0 * degree + 1.0) * points * upper - degree * lower) / (degree + 1.0)
        return ((upper, following), lower)
    carry_end, stacked = lax.scan(emit_row, (jnp.ones_like(points), points), jnp.arange(count, dtype=jnp.int32))
    scale = jnp.sqrt(counter + 0.5)[:, None] * jnp.sqrt(weights)[None, :]
    return (stacked * scale).astype(jnp.bfloat16)

def inverse_moment(indices):
    position = grid_spacing * (indices.astype(jnp.float32) + 1.0)
    return 1.0 / (2.0 * reduced_mass * position * position)

def absorber_keep(region, strength):
    marks = (region[..., None] == jnp.arange(NREGION, dtype=jnp.int32)).astype(jnp.float32)
    strength_cell = lax.optimization_barrier(jnp.sum(marks * strength, axis=-1))
    ramp = (jnp.arange(RABS, dtype=jnp.float32) + 1.0) / RABS
    return jnp.exp(-time_step * strength_cell[..., None] * ramp * ramp)

def finish(new_real, new_imag, keep):
    inner = NS - RABS
    window_real = new_real[..., inner:]
    window_imag = new_imag[..., inner:]
    absorbed = jnp.stack([(1.0 - keep) * window_real, (1.0 - keep) * window_imag])
    state_real = jnp.concatenate([new_real[..., :inner], keep * window_real], axis=-1)
    state_imag = jnp.concatenate([new_imag[..., :inner], keep * window_imag], axis=-1)
    return (jnp.stack([state_real, state_imag]), absorbed)

def add_flux(flux, absorbed, route_owner, route_row, route_weight):
    shaped = absorbed.reshape(2, N_PEN, R_DEV, N_GRP, A_DEV, RABS)
    blocks = shaped.transpose(3, 1, 2, 4, 0, 5).reshape(N_GRP, N_PEN, R_DEV * A_DEV, 2 * RABS)
    group_index = jnp.arange(N_GRP, dtype=jnp.int32)[:, None, None]
    for which_route in range(2):
        flux = flux.at[group_index, route_owner[..., which_route], route_row[..., which_route]].add(blocks * route_weight[..., which_route, None])
    return flux

def reference(psi, potential, absorber_region, absorber_strength, route_owner, route_row, route_weight):
    table_short = sine_table(NS)
    table_long = sine_table(NL).astype(jnp.float32)
    angular = legendre_table(NANG).astype(jnp.float32)
    short_cos, short_sin = kinetic_phase(NS)
    long_cos, long_sin = kinetic_phase(NL)
    order_values = jnp.arange(NANG, dtype=jnp.float32)
    rotor = order_values * (order_values + 1.0)
    inv_short = inverse_moment(jnp.arange(NS, dtype=jnp.int32))
    inv_long = inverse_moment(jnp.arange(NL, dtype=jnp.int32))
    keep = absorber_keep(absorber_region, absorber_strength)
    row_block = math.gcd(NL, 64)
    angle_block = math.gcd(NANG, 16)
    count_rows = NL // row_block
    potential_blocks = potential.reshape(count_rows, row_block, NANG, NS)
    keep_blocks = keep.reshape(count_rows, row_block, NANG, RABS)
    inv_blocks = inv_long.reshape(count_rows, row_block)

    def short_pass(pieces):
        block_state, block_potential = pieces
        cosine = jnp.cos(0.5 * time_step * block_potential)
        sine_part = jnp.sin(0.5 * time_step * block_potential)
        first_real, first_imag = rotate(block_state[0], block_state[1], cosine, sine_part)
        moved = jnp.stack([first_real, first_imag]).astype(jnp.bfloat16)
        coeff = jnp.dot(moved.reshape(-1, NS), table_short, preferred_element_type=jnp.float32).reshape(moved.shape)
        turn_real, turn_imag = rotate(coeff[0], coeff[1], short_cos, short_sin)
        scaled = jnp.stack([turn_real, turn_imag]).astype(jnp.bfloat16)
        done = jnp.dot(scaled.reshape(-1, NS), table_short, preferred_element_type=jnp.float32)
        return done.reshape(moved.shape).astype(jnp.bfloat16)

    def long_pass(block_v):
        coeff = jnp.einsum('mn,cnax->cmax', table_long, block_v.astype(jnp.float32))
        turn_real, turn_imag = rotate(coeff[0], coeff[1], long_cos[:, None, None], long_sin[:, None, None])
        scaled = jnp.stack([turn_real, turn_imag]).astype(jnp.bfloat16)
        return jnp.einsum('mn,cnax->cmax', table_long, scaled.astype(jnp.float32)).astype(jnp.bfloat16)

    def angle_pass(pieces):
        block_w, block_potential, block_inv, block_keep = pieces
        coeff = jnp.einsum('ja,cbax->cbjx', angular, block_w.astype(jnp.float32))
        energy = jnp.minimum(rotor[None, :, None] * (block_inv[:, None, None] + inv_short[None, None, :]), energy_cap)
        turn_real, turn_imag = rotate(coeff[0], coeff[1], jnp.cos(time_step * energy), jnp.sin(time_step * energy))
        scaled = jnp.stack([turn_real, turn_imag]).astype(jnp.bfloat16)
        back = jnp.einsum('ja,cbjx->cbax', angular, scaled.astype(jnp.float32)).astype(jnp.bfloat16)
        widened = lax.optimization_barrier(back).astype(jnp.float32)
        cosine = jnp.cos(0.5 * time_step * block_potential)
        sine_part = jnp.sin(0.5 * time_step * block_potential)
        new_real, new_imag = rotate(widened[0], widened[1], cosine, sine_part)
        return finish(new_real, new_imag, block_keep)
    state = psi
    flux = jnp.zeros((N_GRP, N_PEN, PSROWS, 2 * RABS), jnp.float32)
    for section_index in range(STEPS):
        state_blocks = jnp.moveaxis(state.reshape(2, count_rows, row_block, NANG, NS), 1, 0)
        short_done = lax.map(short_pass, (state_blocks, potential_blocks))
        short_full = jnp.moveaxis(short_done, 0, 1).reshape(2, NL, NANG, NS)
        angle_groups = jnp.moveaxis(short_full.reshape(2, NL, NANG // angle_block, angle_block, NS), 2, 0)
        long_done = lax.map(long_pass, angle_groups)
        long_full = jnp.moveaxis(long_done, 0, 2).reshape(2, NL, NANG, NS)
        row_groups = jnp.moveaxis(long_full.reshape(2, count_rows, row_block, NANG, NS), 1, 0)
        new_blocks, absorbed_blocks = lax.map(angle_pass, (row_groups, potential_blocks, inv_blocks, keep_blocks))
        state = jnp.moveaxis(new_blocks, 0, 1).reshape(2, NL, NANG, NS)
        absorbed = jnp.moveaxis(absorbed_blocks, 0, 1).reshape(2, NL, NANG, RABS)
        flux = add_flux(flux, absorbed, route_owner, route_row, route_weight)
    return (state, flux)
```

```python
import functools
import math

import jax
import jax.numpy as jnp
import ml_dtypes
import numpy as np
from jax import lax
from jax.experimental import pallas as pl
from jax.experimental.pallas import tpu as pltpu
from jax.sharding import PartitionSpec as P

NS = 512
NL = 512
NANG = 128
RABS = 128
STEPS = 2
NREGION = 4
PSROWS = 64


time_step = 0.05
grid_spacing = 0.1
reduced_mass = 0.999456
energy_cap = 500.0


def sine_table(count):
    counter = jnp.arange(count, dtype=jnp.int32) + 1
    product = counter[:, None] * counter[None, :] % (2 * (count + 1))
    angles = jnp.pi * product.astype(jnp.float32) / (count + 1)
    return (math.sqrt(2.0 / (count + 1)) * jnp.sin(angles)).astype(jnp.bfloat16)


def kinetic_phase(count):
    wave = jnp.pi * (jnp.arange(count, dtype=jnp.float32) + 1.0) / (grid_spacing * (count + 1))
    angle_now = time_step * wave * wave / (2.0 * reduced_mass)
    return (jnp.cos(angle_now), jnp.sin(angle_now))


def rotate(real_part, imag_part, cosine, sine_part):
    return (real_part * cosine + imag_part * sine_part, imag_part * cosine - real_part * sine_part)


def legendre_pair(points, count):

    def advance_degree(degree_index, carry):
        previous, current = carry
        degree = degree_index.astype(points.dtype)
        following = ((2.0 * degree + 1.0) * points * current - degree * previous) / (degree + 1.0)
        return (current, following)

    return lax.fori_loop(1, count, advance_degree, (jnp.ones_like(points), points))


def legendre_table(count):
    counter = jnp.arange(count, dtype=jnp.float32)
    points = jnp.cos(jnp.pi * (counter + 0.75) / (count + 0.5))
    for newton_round in range(8):
        previous, current = legendre_pair(points, count)
        slope = count * (points * current - previous) / (points * points - 1.0)
        points = points - current / slope
    previous, current = legendre_pair(points, count)
    slope = count * (points * current - previous) / (points * points - 1.0)
    weights = 2.0 / ((1.0 - points * points) * slope * slope)

    def emit_row(carry, degree_index):
        lower, upper = carry
        degree = degree_index.astype(points.dtype) + 1.0
        following = ((2.0 * degree + 1.0) * points * upper - degree * lower) / (degree + 1.0)
        return ((upper, following), lower)

    carry_end, stacked = lax.scan(
        emit_row, (jnp.ones_like(points), points), jnp.arange(count, dtype=jnp.int32)
    )
    scale = jnp.sqrt(counter + 0.5)[:, None] * jnp.sqrt(weights)[None, :]
    return (stacked * scale).astype(jnp.bfloat16)


def inverse_moment(indices):
    position = grid_spacing * (indices.astype(jnp.float32) + 1.0)
    return 1.0 / (2.0 * reduced_mass * position * position)


def absorber_keep(region, strength):
    marks = (region[..., None] == jnp.arange(NREGION, dtype=jnp.int32)).astype(jnp.float32)
    strength_cell = jnp.sum(marks * strength, axis=-1)
    ramp = (jnp.arange(RABS, dtype=jnp.float32) + 1.0) / RABS
    return jnp.exp(-time_step * strength_cell[..., None] * ramp * ramp)


def finish(new_real, new_imag, keep):
    inner = NS - RABS
    window_real = new_real[..., inner:]
    window_imag = new_imag[..., inner:]
    absorbed = jnp.stack([(1.0 - keep) * window_real, (1.0 - keep) * window_imag])
    state_real = jnp.concatenate([new_real[..., :inner], keep * window_real], axis=-1)
    state_imag = jnp.concatenate([new_imag[..., :inner], keep * window_imag], axis=-1)
    return (jnp.stack([state_real, state_imag]), absorbed)


def route_flux(absorbed, route_owner, route_row, route_weight):
    blocks = absorbed.transpose(1, 2, 0, 3).reshape(-1, 2 * RABS)
    owners = route_owner.reshape(-1)
    targets = route_row.reshape(-1)
    weights = route_weight.reshape(-1)
    pen_count = lax.axis_size("pen")
    capacity = 4 * blocks.shape[0] // pen_count
    entries = jnp.repeat(blocks, 2, axis=0) * weights[:, None]
    marks = (owners[:, None] == jnp.arange(pen_count, dtype=jnp.int32)[None, :]).astype(jnp.int32)
    before = jnp.cumsum(marks, axis=0) - marks
    slots = jnp.sum(before * marks, axis=1)
    send_data = (
        jnp.zeros((pen_count, capacity, 2 * RABS), jnp.float32).at[owners, slots].add(entries)
    )
    send_rows = jnp.zeros((pen_count, capacity), jnp.int32).at[owners, slots].set(targets)
    got_data, got_rows = (
        lax.all_to_all(
            send_data.astype(jnp.bfloat16), "pen", split_axis=0, concat_axis=0, tiled=True
        ).astype(send_data.dtype),
        lax.all_to_all(send_rows, "pen", split_axis=0, concat_axis=0, tiled=True),
    )
    picker = (got_rows.reshape(-1)[None, :] == jnp.arange(PSROWS, dtype=jnp.int32)[:, None]).astype(
        jnp.float32
    )
    return jnp.dot(picker, got_data.reshape(-1, 2 * RABS), precision=lax.Precision.HIGHEST)


def on_device(
    psi, potential, absorber_region, absorber_strength, route_owner, route_row, route_weight
):
    rows_here = psi.shape[1]
    table_short = sine_table(NS)
    table_long = sine_table(NL)
    angular = legendre_table(NANG)
    short_cos, short_sin = kinetic_phase(NS)
    long_cos, long_sin = kinetic_phase(NL)
    order_values = jnp.arange(NANG, dtype=jnp.float32)
    rotor = order_values * (order_values + 1.0)
    half_cos = jnp.cos(0.5 * time_step * potential)
    half_sin = jnp.sin(0.5 * time_step * potential)
    keep = absorber_keep(absorber_region, absorber_strength)
    long_first = lax.axis_index("pen") * rows_here
    long_index = long_first + jnp.arange(rows_here, dtype=jnp.int32)
    state = psi
    flux = jnp.zeros((PSROWS, 2 * RABS), jnp.float32)
    for section_index in range(STEPS):
        first_real, first_imag = rotate(state[0], state[1], half_cos, half_sin)
        moved = jnp.stack([first_real, first_imag]).astype(jnp.bfloat16)
        coeff = jnp.dot(
            moved.reshape(-1, NS), table_short, preferred_element_type=jnp.float32
        ).reshape(moved.shape)
        turn_real, turn_imag = rotate(coeff[0], coeff[1], short_cos, short_sin)
        scaled = jnp.stack([turn_real, turn_imag]).astype(jnp.bfloat16)
        short_done = jnp.dot(
            scaled.reshape(-1, NS), table_short, preferred_element_type=jnp.float32
        )
        short_done = short_done.reshape(moved.shape).astype(jnp.bfloat16)
        long_coeff = jnp.einsum(
            "mn,cnax->cmax",
            table_long,
            lax.all_to_all(short_done, "pen", split_axis=3, concat_axis=1, tiled=True),
            preferred_element_type=jnp.float32,
        )
        long_turn_real, long_turn_imag = rotate(
            long_coeff[0], long_coeff[1], long_cos[:, None, None], long_sin[:, None, None]
        )
        long_scaled = jnp.stack([long_turn_real, long_turn_imag]).astype(jnp.bfloat16)
        long_result = jnp.einsum(
            "mn,cnax->cmax", table_long, long_scaled, preferred_element_type=jnp.float32
        )
        long_done = lax.all_to_all(
            long_result.astype(jnp.bfloat16), "pen", split_axis=1, concat_axis=3, tiled=True
        )
        spread = lax.all_to_all(long_done, "grp", split_axis=3, concat_axis=2, tiled=True)
        width_here = spread.shape[3]
        short_index = lax.axis_index("grp") * width_here + jnp.arange(width_here, dtype=jnp.int32)
        angular_coeff = jnp.einsum(
            "ja,crax->crjx", angular, spread, preferred_element_type=jnp.float32
        )
        energy = jnp.minimum(
            rotor[None, :, None]
            * (
                inverse_moment(long_index)[:, None, None]
                + inverse_moment(short_index)[None, None, :]
            ),
            energy_cap,
        )
        angular_turn_real, angular_turn_imag = rotate(
            angular_coeff[0],
            angular_coeff[1],
            jnp.cos(time_step * energy),
            jnp.sin(time_step * energy),
        )
        angular_scaled = jnp.stack([angular_turn_real, angular_turn_imag]).astype(jnp.bfloat16)
        result = jnp.einsum(
            "ja,crjx->crax", angular, angular_scaled, preferred_element_type=jnp.float32
        )
        turned = result.astype(jnp.bfloat16)
        back = lax.all_to_all(turned, "grp", split_axis=2, concat_axis=3, tiled=True)
        widened = back.astype(jnp.float32)
        new_real, new_imag = rotate(widened[0], widened[1], half_cos, half_sin)
        state, absorbed = finish(new_real, new_imag, keep)
        flux = flux + route_flux(absorbed, route_owner, route_row, route_weight)
    return (state, flux.reshape(1, 1, PSROWS, 2 * RABS))


ROWS = 16
LANES = 128
VMEM = 56 * 1024 * 1024
MESH = pl.DeviceIdType.MESH


def tiles_fit(groups, pens):
    devices = groups * pens
    return (
        NL % (devices * ROWS) == 0
        and NANG % (groups * 32) == 0
        and NANG % devices == 0
        and NS % LANES == 0
        and RABS % LANES == 0
    )


def sine_constant(count):
    counter = np.arange(count, dtype=np.int64) + 1
    product = counter[:, None] * counter[None, :] % (2 * (count + 1))
    table = math.sqrt(2.0 / (count + 1)) * np.sin(np.pi * product / (count + 1))
    return table.astype(np.float32).astype(ml_dtypes.bfloat16)


def phase_constant(count):
    wave = np.pi * (np.arange(count) + 1.0) / (grid_spacing * (count + 1))
    turn = time_step * wave * wave / (2.0 * reduced_mass)
    return np.stack([np.cos(turn), np.sin(turn)]).astype(np.float32)


def legendre_constant(count):
    points = np.cos(np.pi * (np.arange(count) + 0.75) / (count + 0.5))

    def ladder(at):
        rows = [np.ones_like(at), at]
        for degree in range(1, count):
            rows.append(((2.0 * degree + 1.0) * at * rows[-1] - degree * rows[-2]) / (degree + 1.0))
        return rows

    def slope_of(at, rows):
        return count * (at * rows[count] - rows[count - 1]) / (at * at - 1.0)

    for newton_round in range(8):
        rows = ladder(points)
        points = points - rows[count] / slope_of(points, rows)
    rows = ladder(points)
    weights = 2.0 / ((1.0 - points * points) * slope_of(points, rows) ** 2)
    table = np.sqrt(np.arange(count) + 0.5)[:, None] * np.sqrt(weights)[None, :] * np.stack(rows[:count])
    return table.astype(np.float32).astype(ml_dtypes.bfloat16)


def small_turn(potential):
    x = (0.5 * time_step) * potential
    q = x * x
    cosine = 1.0 + q * (-1.0 / 2 + q * (1.0 / 24 + q * (-1.0 / 720 + q * (1.0 / 40320))))
    sine = x * (1.0 + q * (-1.0 / 6 + q * (1.0 / 120 + q * (-1.0 / 5040 + q * (1.0 / 362880)))))
    return cosine, sine


def wide_turn(angle):
    turns = angle * (0.5 / math.pi)
    half = (turns - jnp.round(turns)) * math.pi
    q = half * half
    c = 1.0 + q * (
        -1.0 / 2
        + q * (1.0 / 24 + q * (-1.0 / 720 + q * (1.0 / 40320 + q * (-1.0 / 3628800 + q / 479001600.0))))
    )
    s = half * (
        1.0
        + q * (-1.0 / 6 + q * (1.0 / 120 + q * (-1.0 / 5040 + q * (1.0 / 362880 - q / 39916800.0))))
    )
    return 1.0 - 2.0 * s * s, 2.0 * s * c


def short_kernel(first, last, *refs):
    refs = list(refs)
    wave_ref, pot_ref = refs.pop(0), refs.pop(0)
    keep_ref = None if first else refs.pop(0)
    if not last:
        table_ref, phase_ref = refs.pop(0), refs.pop(0)
    psi_ref = refs.pop(0) if last else None
    lost_ref = None if first else refs.pop(0)
    if not last:
        out_ref, stage = refs.pop(0), refs.pop(0)
    angles = pot_ref.shape[1]
    inner = NS - RABS
    batch = 4

    def rows(h, carry):
        parts_real, parts_imag = [], []
        for k in range(batch):
            r = h * batch + k
            half_cos, half_sin = small_turn(pot_ref[r])
            if first:
                real, imag = wave_ref[0, r], wave_ref[1, r]
            else:
                real = wave_ref[r, 0].astype(jnp.float32)
                imag = wave_ref[r, 1].astype(jnp.float32)
                real, imag = rotate(real, imag, half_cos, half_sin)
                keep = keep_ref[r]
                tail_real, tail_imag = real[:, inner:], imag[:, inner:]
                kept_real, kept_imag = keep * tail_real, keep * tail_imag
                lost_ref[r, :, :RABS] = (tail_real - kept_real).astype(jnp.bfloat16)
                lost_ref[r, :, RABS:] = (tail_imag - kept_imag).astype(jnp.bfloat16)
                real = jnp.concatenate([real[:, :inner], kept_real], axis=-1)
                imag = jnp.concatenate([imag[:, :inner], kept_imag], axis=-1)
            if last:
                psi_ref[0, r] = real
                psi_ref[1, r] = imag
            else:
                real, imag = rotate(real, imag, half_cos, half_sin)
                parts_real.append(real.astype(jnp.bfloat16))
                parts_imag.append(imag.astype(jnp.bfloat16))
        if not last:
            lines = batch * angles
            both = jnp.concatenate(parts_real + parts_imag, axis=0)
            coeff = jnp.dot(both, table_ref[...], preferred_element_type=jnp.float32)
            real, imag = rotate(coeff[:lines], coeff[lines:], phase_ref[0:1], phase_ref[1:2])
            both = jnp.concatenate([real.astype(jnp.bfloat16), imag.astype(jnp.bfloat16)], axis=0)
            done = jnp.dot(both, table_ref[...], preferred_element_type=jnp.float32)
            for q in range(NS // LANES):
                at = pl.ds(pl.multiple_of(h * lines, lines), lines)
                stage[0, q, at, :] = done[:lines, q * LANES : (q + 1) * LANES]
                stage[1, q, at, :] = done[lines:, q * LANES : (q + 1) * LANES]
        return carry

    lax.fori_loop(0, ROWS // batch, rows, 0)
    if not last:
        for a in range(angles):
            for c in range(2):
                for q in range(NS // LANES):
                    picked = stage[c, q, pl.ds(a, ROWS, stride=angles), :]
                    out_ref[a, c, :, q * LANES : (q + 1) * LANES] = picked.astype(jnp.bfloat16)


def short_pass(first, last, wave, potential, keep, table, phase):
    here, angles = potential.shape[:2]
    if first:
        wave_spec = pl.BlockSpec((2, ROWS, angles, NS), lambda i: (0, i, 0, 0))
    else:
        wave_spec = pl.BlockSpec((ROWS, 2, angles, NS), lambda i: (i, 0, 0, 0))
    ins = [wave, potential]
    in_specs = [wave_spec, pl.BlockSpec((ROWS, angles, NS), lambda i: (i, 0, 0))]
    outs, out_specs, scratch = [], [], []
    if not first:
        ins.append(keep)
        in_specs.append(pl.BlockSpec((ROWS, angles, RABS), lambda i: (i, 0, 0)))
    if last:
        outs.append(jax.ShapeDtypeStruct((2, here, angles, NS), jnp.float32))
        out_specs.append(pl.BlockSpec((2, ROWS, angles, NS), lambda i: (0, i, 0, 0)))
    else:
        ins += [table, phase]
        in_specs += [
            pl.BlockSpec((NS, NS), lambda i: (0, 0)),
            pl.BlockSpec((2, NS), lambda i: (0, 0)),
        ]
    if not first:
        outs.append(jax.ShapeDtypeStruct((here, angles, 2 * RABS), jnp.bfloat16))
        out_specs.append(pl.BlockSpec((ROWS, angles, 2 * RABS), lambda i: (i, 0, 0)))
    if not last:
        outs.append(jax.ShapeDtypeStruct((angles, 2, here, NS), jnp.bfloat16))
        out_specs.append(pl.BlockSpec((angles, 2, ROWS, NS), lambda i: (0, 0, i, 0)))
        scratch.append(pltpu.VMEM((2, NS // LANES, ROWS * angles, LANES), jnp.float32))
    return pl.pallas_call(
        functools.partial(short_kernel, first, last),
        grid=(here // ROWS,),
        in_specs=in_specs,
        out_specs=out_specs,
        out_shape=outs,
        scratch_shapes=scratch,
        compiler_params=pltpu.CompilerParams(vmem_limit_bytes=VMEM),
        name="short_first" if first else "short_last" if last else "short_mid",
    )(*ins)


def long_kernel(groups, pens, wave_ref, table_ref, cos_ref, sin_ref, out_ref):
    table = table_ref[...]
    tile = 2 * LANES
    rows = out_ref.shape[4]

    def columns(q, carry):
        at = pl.ds(pl.multiple_of(q * tile, tile), tile)
        coeff = [
            jnp.dot(
                table,
                wave_ref[:, 0, c, :, at].reshape(NL, tile),
                preferred_element_type=jnp.float32,
            )
            for c in range(2)
        ]
        cosine = jnp.concatenate([cos_ref[...]] * 2, axis=1)
        sine = jnp.concatenate([sin_ref[...]] * 2, axis=1)
        turned = rotate(coeff[0], coeff[1], cosine, sine)
        for c in range(2):
            done = jnp.dot(table, turned[c].astype(jnp.bfloat16), preferred_element_type=jnp.float32)
            done = done.astype(jnp.bfloat16).reshape(pens, groups, rows, tile)
            for g in range(groups):
                out_ref[g, :, 0, c, :, at] = done[:, g]
        return carry

    lax.fori_loop(0, NS // tile, columns, 0)


def long_pass(groups, wave, table, cosine, sine):
    pens, angles, _, here, _ = wave.shape
    rows = here // groups
    return pl.pallas_call(
        functools.partial(long_kernel, groups, pens),
        grid=(angles,),
        in_specs=[
            pl.BlockSpec((pens, 1, 2, here, NS), lambda i: (0, i, 0, 0, 0)),
            pl.BlockSpec((NL, NL), lambda i: (0, 0)),
            pl.BlockSpec((NL, LANES), lambda i: (0, 0)),
            pl.BlockSpec((NL, LANES), lambda i: (0, 0)),
        ],
        out_specs=pl.BlockSpec((groups, pens, 1, 2, rows, NS), lambda i: (0, 0, i, 0, 0, 0)),
        out_shape=jax.ShapeDtypeStruct((groups, pens, angles, 2, rows, NS), jnp.bfloat16),
        compiler_params=pltpu.CompilerParams(vmem_limit_bytes=VMEM),
        name="long_pass",
    )(wave, table, cosine, sine)


def angle_kernel(wave_ref, table_ref, table_t_ref, inv_long_ref, inv_short_ref, rotor_ref, out_ref, stage):
    rows = out_ref.shape[1]
    groups, share = out_ref.shape[0], out_ref.shape[3]
    stage[...] = wave_ref[...].reshape(stage.shape).astype(jnp.float32)
    rotor = rotor_ref[...]

    def one(r):
        both = jnp.concatenate(
            [stage[pl.ds(c * rows + r, NANG, stride=2 * rows), :] for c in range(2)], axis=1
        ).astype(jnp.bfloat16)
        coeff = jnp.dot(table_ref[...], both, preferred_element_type=jnp.float32)
        moment = inv_long_ref[pl.ds(r, 1), :] + inv_short_ref[...]
        cosine, sine = wide_turn(time_step * jnp.minimum(rotor * moment, energy_cap))
        real, imag = rotate(coeff[:, :LANES], coeff[:, LANES:], cosine, sine)
        both = jnp.concatenate([real, imag], axis=1).astype(jnp.bfloat16)
        done = jnp.dot(table_t_ref[...], both, preferred_element_type=jnp.float32).astype(jnp.bfloat16)
        for g in range(groups):
            for c in range(2):
                out_ref[g, r, c] = done[g * share : (g + 1) * share, c * LANES : (c + 1) * LANES]

    def four(k, carry):
        for m in range(4):
            one(k * 4 + m)
        return carry

    lax.fori_loop(0, rows // 4, four, 0)


def angle_pass(groups, wave, table, table_t, inv_long, inv_short, rotor):
    rows = wave.shape[2]
    share = NANG // groups
    return pl.pallas_call(
        angle_kernel,
        grid=(NS // LANES,),
        in_specs=[
            pl.BlockSpec((NANG, 2, rows, LANES), lambda i: (0, 0, 0, i)),
            pl.BlockSpec((NANG, NANG), lambda i: (0, 0)),
            pl.BlockSpec((NANG, NANG), lambda i: (0, 0)),
            pl.BlockSpec((rows, LANES), lambda i: (0, 0)),
            pl.BlockSpec((1, LANES), lambda i: (0, i)),
            pl.BlockSpec((NANG, LANES), lambda i: (0, 0)),
        ],
        out_specs=pl.BlockSpec((groups, rows, 2, share, LANES), lambda i: (0, 0, 0, 0, i)),
        out_shape=jax.ShapeDtypeStruct((groups, rows, 2, share, NS), jnp.bfloat16),
        scratch_shapes=[pltpu.VMEM((NANG * 2 * rows, LANES), jnp.float32)],
        compiler_params=pltpu.CompilerParams(vmem_limit_bytes=VMEM),
        name="angle_pass",
    )(wave, table, table_t, inv_long, inv_short, rotor)


def exchange_kernel(groups, pens, x_ref, o_ref, send_sem, recv_sem, local_sem):
    g, p = lax.axis_index("grp"), lax.axis_index("pen")
    wide_g, wide_p = groups > 1, pens > 1
    count_g, count_p = lax.axis_size("grp"), lax.axis_size("pen")
    partners = [(dg, dp) for dg in range(groups) for dp in range(pens) if (dg, dp) != (0, 0)]
    partners.sort(key=lambda q: -((q[0] != 0) + (q[1] != 0)))

    def place(gg, pp):
        return (gg * pens if wide_g else 0) + (pp if wide_p else 0)

    def target(q):
        return lax.rem(g + q[0], count_g), lax.rem(p + q[1], count_p)

    barrier = pltpu.get_barrier_semaphore()
    for q in partners:
        pl.semaphore_signal(barrier, inc=1, device_id=target(q), device_id_type=MESH)
    pl.semaphore_wait(barrier, len(partners))
    me = place(g, p)
    copies = []
    for k, q in enumerate(partners):
        to = target(q)
        copy = pltpu.make_async_remote_copy(
            src_ref=x_ref.at[place(*to)],
            dst_ref=o_ref.at[me],
            send_sem=send_sem.at[k],
            recv_sem=recv_sem.at[k],
            device_id=to,
            device_id_type=MESH,
        )
        copy.start()
        copies.append(copy)
    local = pltpu.make_async_copy(x_ref.at[me], o_ref.at[me], local_sem)
    local.start()
    local.wait()
    for copy in copies:
        copy.wait()


def exchange(x, groups, pens, collective_id):
    count = groups * pens
    return pl.pallas_call(
        functools.partial(exchange_kernel, groups, pens),
        out_shape=jax.ShapeDtypeStruct(x.shape, x.dtype),
        in_specs=[pl.BlockSpec(memory_space=pl.ANY)],
        out_specs=pl.BlockSpec(memory_space=pl.ANY),
        scratch_shapes=[
            pltpu.SemaphoreType.DMA((count - 1,)),
            pltpu.SemaphoreType.DMA((count - 1,)),
            pltpu.SemaphoreType.DMA,
        ],
        compiler_params=pltpu.CompilerParams(collective_id=collective_id, has_side_effects=True),
        name="exchange_%d" % collective_id,
    )(x)


def route_matrix(route_owner, route_row, route_weight, pens):
    lines = route_owner.shape[2]
    keys = (route_owner * PSROWS + route_row).reshape(lines, 2)
    weights = route_weight.reshape(lines, 2)
    targets = jnp.arange(pens * PSROWS, dtype=jnp.int32)[:, None]
    total = jnp.zeros((pens * PSROWS, lines), jnp.float32)
    for k in range(2):
        total = total + jnp.where(targets == keys[None, :, k], weights[None, :, k], 0.0)
    return total.astype(jnp.bfloat16)


def on_device_tiled(
    psi, potential, absorber_region, absorber_strength, route_owner, route_row, route_weight
):
    groups, pens = lax.axis_size("grp"), lax.axis_size("pen")
    here, angles = potential.shape[:2]
    rows = here // groups
    share = NANG // (groups * pens)
    table_short = jnp.asarray(sine_constant(NS))
    table_long = jnp.asarray(sine_constant(NL))
    angular_np = legendre_constant(NANG)
    angular, angular_t = jnp.asarray(angular_np), jnp.asarray(angular_np.T)
    short_phase = jnp.asarray(phase_constant(NS))
    long_phase = phase_constant(NL)
    long_cos = jnp.broadcast_to(jnp.asarray(long_phase[0])[:, None], (NL, LANES))
    long_sin = jnp.broadcast_to(jnp.asarray(long_phase[1])[:, None], (NL, LANES))
    order = jnp.arange(NANG, dtype=jnp.float32)
    rotor = jnp.broadcast_to((order * (order + 1.0))[:, None], (NANG, LANES))
    first_row = lax.axis_index("pen") * here + lax.axis_index("grp") * rows
    inv_long = inverse_moment(first_row + jnp.arange(rows, dtype=jnp.int32))
    inv_long = jnp.broadcast_to(inv_long[:, None], (rows, LANES))
    inv_short = inverse_moment(jnp.arange(NS, dtype=jnp.int32))[None, :]
    keep = absorber_keep(absorber_region, absorber_strength)
    routes = route_matrix(route_owner, route_row, route_weight, pens)

    flux = jnp.zeros((pens * PSROWS, 2 * RABS), jnp.float32)
    (wave,) = short_pass(True, False, psi, potential, keep, table_short, short_phase)
    for step in range(STEPS):
        wave = exchange(wave.reshape(pens, share, 2, here, NS), 1, pens, 1)
        wave = long_pass(groups, wave, table_long, long_cos, long_sin)
        wave = exchange(wave.reshape(groups * pens, share, 2, rows, NS), groups, pens, 2)
        wave = angle_pass(
            groups, wave.reshape(NANG, 2, rows, NS), angular, angular_t, inv_long, inv_short, rotor
        )
        wave = exchange(wave, groups, 1, 3).reshape(here, 2, angles, NS)
        if step + 1 < STEPS:
            lost, wave = short_pass(False, False, wave, potential, keep, table_short, short_phase)
        else:
            state, lost = short_pass(False, True, wave, potential, keep, table_short, short_phase)
        flux = flux + jnp.dot(
            routes, lost.reshape(here * angles, 2 * RABS), preferred_element_type=jnp.float32
        )
    parts = lax.all_to_all(flux.reshape(pens, PSROWS, 2 * RABS), "pen", 0, 0, tiled=True)
    return (state, jnp.sum(parts, axis=0).reshape(1, 1, PSROWS, 2 * RABS))


def solution(mesh):
    groups, pens = mesh.shape["grp"], mesh.shape["pen"]
    body = on_device_tiled if tiles_fit(groups, pens) else on_device
    return jax.shard_map(
        body,
        mesh=mesh,
        in_specs=(
            P(None, "pen", "grp", None),
            P("pen", "grp", None),
            P("pen", "grp"),
            P(),
            P("grp", "pen", None, None),
            P("grp", "pen", None, None),
            P("grp", "pen", None, None),
        ),
        out_specs=(P(None, "pen", "grp", None), P("grp", "pen", None, None)),
        check_vma=False,
    )
```

```python
import functools
import math

import jax
import jax.numpy as jnp
import ml_dtypes
import numpy as np
from jax import lax
from jax.experimental import pallas as pl
from jax.experimental.pallas import tpu as pltpu
from jax.sharding import PartitionSpec as P

NS = 512
NL = 512
NANG = 128
RABS = 128
STEPS = 2
NREGION = 4
PSROWS = 64


time_step = 0.05
grid_spacing = 0.1
reduced_mass = 0.999456
energy_cap = 500.0


def sine_table(count):
    counter = jnp.arange(count, dtype=jnp.int32) + 1
    product = counter[:, None] * counter[None, :] % (2 * (count + 1))
    angles = jnp.pi * product.astype(jnp.float32) / (count + 1)
    return (math.sqrt(2.0 / (count + 1)) * jnp.sin(angles)).astype(jnp.bfloat16)


def kinetic_phase(count):
    wave = jnp.pi * (jnp.arange(count, dtype=jnp.float32) + 1.0) / (grid_spacing * (count + 1))
    angle_now = time_step * wave * wave / (2.0 * reduced_mass)
    return (jnp.cos(angle_now), jnp.sin(angle_now))


def rotate(real_part, imag_part, cosine, sine_part):
    return (real_part * cosine + imag_part * sine_part, imag_part * cosine - real_part * sine_part)


def legendre_pair(points, count):

    def advance_degree(degree_index, carry):
        previous, current = carry
        degree = degree_index.astype(points.dtype)
        following = ((2.0 * degree + 1.0) * points * current - degree * previous) / (degree + 1.0)
        return (current, following)

    return lax.fori_loop(1, count, advance_degree, (jnp.ones_like(points), points))


def legendre_table(count):
    counter = jnp.arange(count, dtype=jnp.float32)
    points = jnp.cos(jnp.pi * (counter + 0.75) / (count + 0.5))
    for newton_round in range(8):
        previous, current = legendre_pair(points, count)
        slope = count * (points * current - previous) / (points * points - 1.0)
        points = points - current / slope
    previous, current = legendre_pair(points, count)
    slope = count * (points * current - previous) / (points * points - 1.0)
    weights = 2.0 / ((1.0 - points * points) * slope * slope)

    def emit_row(carry, degree_index):
        lower, upper = carry
        degree = degree_index.astype(points.dtype) + 1.0
        following = ((2.0 * degree + 1.0) * points * upper - degree * lower) / (degree + 1.0)
        return ((upper, following), lower)

    carry_end, stacked = lax.scan(
        emit_row, (jnp.ones_like(points), points), jnp.arange(count, dtype=jnp.int32)
    )
    scale = jnp.sqrt(counter + 0.5)[:, None] * jnp.sqrt(weights)[None, :]
    return (stacked * scale).astype(jnp.bfloat16)


def inverse_moment(indices):
    position = grid_spacing * (indices.astype(jnp.float32) + 1.0)
    return 1.0 / (2.0 * reduced_mass * position * position)


def absorber_keep(region, strength):
    marks = (region[..., None] == jnp.arange(NREGION, dtype=jnp.int32)).astype(jnp.float32)
    strength_cell = jnp.sum(marks * strength, axis=-1)
    ramp = (jnp.arange(RABS, dtype=jnp.float32) + 1.0) / RABS
    return jnp.exp(-time_step * strength_cell[..., None] * ramp * ramp)


def finish(new_real, new_imag, keep):
    inner = NS - RABS
    window_real = new_real[..., inner:]
    window_imag = new_imag[..., inner:]
    absorbed = jnp.stack([(1.0 - keep) * window_real, (1.0 - keep) * window_imag])
    state_real = jnp.concatenate([new_real[..., :inner], keep * window_real], axis=-1)
    state_imag = jnp.concatenate([new_imag[..., :inner], keep * window_imag], axis=-1)
    return (jnp.stack([state_real, state_imag]), absorbed)


def route_flux(absorbed, route_owner, route_row, route_weight):
    blocks = absorbed.transpose(1, 2, 0, 3).reshape(-1, 2 * RABS)
    owners = route_owner.reshape(-1)
    targets = route_row.reshape(-1)
    weights = route_weight.reshape(-1)
    pen_count = lax.axis_size("pen")
    capacity = 4 * blocks.shape[0] // pen_count
    entries = jnp.repeat(blocks, 2, axis=0) * weights[:, None]
    marks = (owners[:, None] == jnp.arange(pen_count, dtype=jnp.int32)[None, :]).astype(jnp.int32)
    before = jnp.cumsum(marks, axis=0) - marks
    slots = jnp.sum(before * marks, axis=1)
    send_data = (
        jnp.zeros((pen_count, capacity, 2 * RABS), jnp.float32).at[owners, slots].add(entries)
    )
    send_rows = jnp.zeros((pen_count, capacity), jnp.int32).at[owners, slots].set(targets)
    got_data, got_rows = (
        lax.all_to_all(
            send_data.astype(jnp.bfloat16), "pen", split_axis=0, concat_axis=0, tiled=True
        ).astype(send_data.dtype),
        lax.all_to_all(send_rows, "pen", split_axis=0, concat_axis=0, tiled=True),
    )
    picker = (got_rows.reshape(-1)[None, :] == jnp.arange(PSROWS, dtype=jnp.int32)[:, None]).astype(
        jnp.float32
    )
    return jnp.dot(picker, got_data.reshape(-1, 2 * RABS), precision=lax.Precision.HIGHEST)


def on_device(
    psi, potential, absorber_region, absorber_strength, route_owner, route_row, route_weight
):
    rows_here = psi.shape[1]
    table_short = sine_table(NS)
    table_long = sine_table(NL)
    angular = legendre_table(NANG)
    short_cos, short_sin = kinetic_phase(NS)
    long_cos, long_sin = kinetic_phase(NL)
    order_values = jnp.arange(NANG, dtype=jnp.float32)
    rotor = order_values * (order_values + 1.0)
    half_cos = jnp.cos(0.5 * time_step * potential)
    half_sin = jnp.sin(0.5 * time_step * potential)
    keep = absorber_keep(absorber_region, absorber_strength)
    long_first = lax.axis_index("pen") * rows_here
    long_index = long_first + jnp.arange(rows_here, dtype=jnp.int32)
    state = psi
    flux = jnp.zeros((PSROWS, 2 * RABS), jnp.float32)
    for section_index in range(STEPS):
        first_real, first_imag = rotate(state[0], state[1], half_cos, half_sin)
        moved = jnp.stack([first_real, first_imag]).astype(jnp.bfloat16)
        coeff = jnp.dot(
            moved.reshape(-1, NS), table_short, preferred_element_type=jnp.float32
        ).reshape(moved.shape)
        turn_real, turn_imag = rotate(coeff[0], coeff[1], short_cos, short_sin)
        scaled = jnp.stack([turn_real, turn_imag]).astype(jnp.bfloat16)
        short_done = jnp.dot(
            scaled.reshape(-1, NS), table_short, preferred_element_type=jnp.float32
        )
        short_done = short_done.reshape(moved.shape).astype(jnp.bfloat16)
        long_coeff = jnp.einsum(
            "mn,cnax->cmax",
            table_long,
            lax.all_to_all(short_done, "pen", split_axis=3, concat_axis=1, tiled=True),
            preferred_element_type=jnp.float32,
        )
        long_turn_real, long_turn_imag = rotate(
            long_coeff[0], long_coeff[1], long_cos[:, None, None], long_sin[:, None, None]
        )
        long_scaled = jnp.stack([long_turn_real, long_turn_imag]).astype(jnp.bfloat16)
        long_result = jnp.einsum(
            "mn,cnax->cmax", table_long, long_scaled, preferred_element_type=jnp.float32
        )
        long_done = lax.all_to_all(
            long_result.astype(jnp.bfloat16), "pen", split_axis=1, concat_axis=3, tiled=True
        )
        spread = lax.all_to_all(long_done, "grp", split_axis=3, concat_axis=2, tiled=True)
        width_here = spread.shape[3]
        short_index = lax.axis_index("grp") * width_here + jnp.arange(width_here, dtype=jnp.int32)
        angular_coeff = jnp.einsum(
            "ja,crax->crjx", angular, spread, preferred_element_type=jnp.float32
        )
        energy = jnp.minimum(
            rotor[None, :, None]
            * (
                inverse_moment(long_index)[:, None, None]
                + inverse_moment(short_index)[None, None, :]
            ),
            energy_cap,
        )
        angular_turn_real, angular_turn_imag = rotate(
            angular_coeff[0],
            angular_coeff[1],
            jnp.cos(time_step * energy),
            jnp.sin(time_step * energy),
        )
        angular_scaled = jnp.stack([angular_turn_real, angular_turn_imag]).astype(jnp.bfloat16)
        result = jnp.einsum(
            "ja,crjx->crax", angular, angular_scaled, preferred_element_type=jnp.float32
        )
        turned = result.astype(jnp.bfloat16)
        back = lax.all_to_all(turned, "grp", split_axis=2, concat_axis=3, tiled=True)
        widened = back.astype(jnp.float32)
        new_real, new_imag = rotate(widened[0], widened[1], half_cos, half_sin)
        state, absorbed = finish(new_real, new_imag, keep)
        flux = flux + route_flux(absorbed, route_owner, route_row, route_weight)
    return (state, flux.reshape(1, 1, PSROWS, 2 * RABS))


ROWS = 16
LANES = 128
PAD = 8
VMEM = 56 * 1024 * 1024
MESH = pl.DeviceIdType.MESH


def tiles_fit(groups, pens):
    devices = groups * pens
    return (
        NL % (devices * ROWS) == 0
        and NANG % (groups * 32) == 0
        and NANG % devices == 0
        and NS % LANES == 0
        and RABS % LANES == 0
    )


def sine_constant(count):
    counter = np.arange(count, dtype=np.int64) + 1
    product = counter[:, None] * counter[None, :] % (2 * (count + 1))
    table = math.sqrt(2.0 / (count + 1)) * np.sin(np.pi * product / (count + 1))
    return table.astype(np.float32).astype(ml_dtypes.bfloat16)


def phase_constant(count):
    wave = np.pi * (np.arange(count) + 1.0) / (grid_spacing * (count + 1))
    turn = time_step * wave * wave / (2.0 * reduced_mass)
    return np.stack([np.cos(turn), np.sin(turn)]).astype(np.float32)


def legendre_constant(count):
    points = np.cos(np.pi * (np.arange(count) + 0.75) / (count + 0.5))

    def ladder(at):
        rows = [np.ones_like(at), at]
        for degree in range(1, count):
            rows.append(((2.0 * degree + 1.0) * at * rows[-1] - degree * rows[-2]) / (degree + 1.0))
        return rows

    def slope_of(at, rows):
        return count * (at * rows[count] - rows[count - 1]) / (at * at - 1.0)

    for newton_round in range(8):
        rows = ladder(points)
        points = points - rows[count] / slope_of(points, rows)
    rows = ladder(points)
    weights = 2.0 / ((1.0 - points * points) * slope_of(points, rows) ** 2)
    table = np.sqrt(np.arange(count) + 0.5)[:, None] * np.sqrt(weights)[None, :] * np.stack(rows[:count])
    return table.astype(np.float32).astype(ml_dtypes.bfloat16)


def small_turn(potential):
    x = (0.5 * time_step) * potential
    q = x * x
    cosine = 1.0 + q * (-1.0 / 2 + q * (1.0 / 24 + q * (-1.0 / 720 + q * (1.0 / 40320))))
    sine = x * (1.0 + q * (-1.0 / 6 + q * (1.0 / 120 + q * (-1.0 / 5040 + q * (1.0 / 362880)))))
    return cosine, sine


def wide_turn(angle):
    turns = angle * (0.5 / math.pi)
    half = (turns - jnp.round(turns)) * math.pi
    q = half * half
    c = 1.0 + q * (
        -1.0 / 2
        + q * (1.0 / 24 + q * (-1.0 / 720 + q * (1.0 / 40320 + q * (-1.0 / 3628800 + q / 479001600.0))))
    )
    s = half * (
        1.0
        + q * (-1.0 / 6 + q * (1.0 / 120 + q * (-1.0 / 5040 + q * (1.0 / 362880 - q / 39916800.0))))
    )
    return 1.0 - 2.0 * s * s, 2.0 * s * c


def greet(targets):
    barrier = pltpu.get_barrier_semaphore()
    for to in targets:
        pl.semaphore_signal(barrier, inc=1, device_id=to, device_id_type=MESH)
    pl.semaphore_wait(barrier, len(targets))


def chunk_copies(chunk, me, source, landing, targets, spots, send_sem, recv_sem):
    return [
        pltpu.make_async_remote_copy(
            src_ref=source(chunk, spot),
            dst_ref=landing(chunk, me),
            send_sem=send_sem.at[chunk, k],
            recv_sem=recv_sem.at[chunk, k],
            device_id=to,
            device_id_type=MESH,
        )
        for k, (to, spot) in enumerate(zip(targets, spots))
    ]


def send_chunk(chunk, chunks, me, source, landing, targets, spots, send_sem, recv_sem, local_sem):
    for copy in chunk_copies(chunk, me, source, landing, targets, spots, send_sem, recv_sem):
        copy.start()
    pltpu.make_async_copy(source(chunk, me), landing(chunk, me), local_sem.at[chunk]).start()

    @pl.when(chunk == chunks - 1)
    def _():
        for part in range(chunks):
            for copy in chunk_copies(part, me, source, landing, targets, spots, send_sem, recv_sem):
                copy.wait()
            pltpu.make_async_copy(source(part, me), landing(part, me), local_sem.at[part]).wait()


def short_kernel(first, last, pens, chunks, *refs):
    refs = list(refs)
    wave_ref, pot_ref = refs.pop(0), refs.pop(0)
    keep_ref = None if first else refs.pop(0)
    if not last:
        table_ref, phase_ref = refs.pop(0), refs.pop(0)
    psi_ref = refs.pop(0) if last else None
    lost_ref = None if first else refs.pop(0)
    if not last:
        out_ref, stage, blocks, send_sem, recv_sem, local_sem = refs
        chunk = pl.program_id(0)
        g, p = lax.axis_index("grp"), lax.axis_index("pen")
        spots = [lax.rem(p + d, pens) for d in range(1, pens)]
        targets = [(g, spot) for spot in spots]

        @pl.when(chunk == 0)
        def _():
            greet(targets)

    angles = pot_ref.shape[1]
    inner = NS - RABS
    batch = 4

    def rows(h, carry):
        parts_real, parts_imag = [], []
        for k in range(batch):
            r = h * batch + k
            half_cos, half_sin = small_turn(pot_ref[r])
            if first:
                real, imag = wave_ref[0, r], wave_ref[1, r]
            else:
                real = wave_ref[r, 0].astype(jnp.float32)
                imag = wave_ref[r, 1].astype(jnp.float32)
                real, imag = rotate(real, imag, half_cos, half_sin)
                keep = keep_ref[r]
                tail_real, tail_imag = real[:, inner:], imag[:, inner:]
                kept_real, kept_imag = keep * tail_real, keep * tail_imag
                lost_ref[r, :, :RABS] = (tail_real - kept_real).astype(jnp.bfloat16)
                lost_ref[r, :, RABS:] = (tail_imag - kept_imag).astype(jnp.bfloat16)
                real = jnp.concatenate([real[:, :inner], kept_real], axis=-1)
                imag = jnp.concatenate([imag[:, :inner], kept_imag], axis=-1)
            if last:
                psi_ref[0, r] = real
                psi_ref[1, r] = imag
            else:
                real, imag = rotate(real, imag, half_cos, half_sin)
                parts_real.append(real.astype(jnp.bfloat16))
                parts_imag.append(imag.astype(jnp.bfloat16))
        if not last:
            lines = batch * angles
            both = jnp.concatenate(parts_real + parts_imag, axis=0)
            coeff = jnp.dot(both, table_ref[...], preferred_element_type=jnp.float32)
            real, imag = rotate(coeff[:lines], coeff[lines:], phase_ref[0:1], phase_ref[1:2])
            both = jnp.concatenate([real.astype(jnp.bfloat16), imag.astype(jnp.bfloat16)], axis=0)
            done = jnp.dot(both, table_ref[...], preferred_element_type=jnp.float32)
            pitch = angles + PAD
            for k in range(batch):
                at = pl.ds(pl.multiple_of((h * batch + k) * pitch, 8), angles)
                for c in range(2):
                    for q in range(NS // LANES):
                        first_line = c * lines + k * angles
                        stage[c, q, at, :] = done[
                            first_line : first_line + angles, q * LANES : (q + 1) * LANES
                        ]
        return carry

    lax.fori_loop(0, ROWS // batch, rows, 0)
    if not last:
        for a in range(angles):
            for c in range(2):
                for q in range(NS // LANES):
                    picked = stage[c, q, pl.ds(a, ROWS, stride=angles + PAD), :]
                    to, at = divmod(a, angles // pens)
                    blocks[chunk, to, at, c, :, q * LANES : (q + 1) * LANES] = picked.astype(
                        jnp.bfloat16
                    )

        def source(part, spot):
            return blocks.at[part, spot]

        def landing(part, spot):
            start = part * ROWS if isinstance(part, int) else pl.multiple_of(part * ROWS, ROWS)
            return out_ref.at[spot, :, :, pl.ds(start, ROWS), :]

        send_chunk(
            chunk, chunks, p, source, landing, targets, spots, send_sem, recv_sem, local_sem
        )


def short_pass(first, last, pens, wave, potential, keep, table, phase):
    here, angles = potential.shape[:2]
    if first:
        wave_spec = pl.BlockSpec((2, ROWS, angles, NS), lambda i: (0, i, 0, 0))
    else:
        wave_spec = pl.BlockSpec((ROWS, 2, angles, NS), lambda i: (i, 0, 0, 0))
    ins = [wave, potential]
    in_specs = [wave_spec, pl.BlockSpec((ROWS, angles, NS), lambda i: (i, 0, 0))]
    outs, out_specs, scratch = [], [], []
    if not first:
        ins.append(keep)
        in_specs.append(pl.BlockSpec((ROWS, angles, RABS), lambda i: (i, 0, 0)))
    if last:
        outs.append(jax.ShapeDtypeStruct((2, here, angles, NS), jnp.float32))
        out_specs.append(pl.BlockSpec((2, ROWS, angles, NS), lambda i: (0, i, 0, 0)))
    else:
        ins += [table, phase]
        in_specs += [
            pl.BlockSpec((NS, NS), lambda i: (0, 0)),
            pl.BlockSpec((2, NS), lambda i: (0, 0)),
        ]
    if not first:
        outs.append(jax.ShapeDtypeStruct((here, angles, 2 * RABS), jnp.bfloat16))
        out_specs.append(pl.BlockSpec((ROWS, angles, 2 * RABS), lambda i: (i, 0, 0)))
    if not last:
        share, chunks = angles // pens, here // ROWS
        outs.append(jax.ShapeDtypeStruct((pens, share, 2, here, NS), jnp.bfloat16))
        out_specs.append(pl.BlockSpec(memory_space=pl.ANY))
        scratch.append(pltpu.VMEM((2, NS // LANES, ROWS * (angles + PAD), LANES), jnp.float32))
        scratch.append(pltpu.VMEM((chunks, pens, share, 2, ROWS, NS), jnp.bfloat16))
        scratch.append(pltpu.SemaphoreType.DMA((chunks, pens - 1)))
        scratch.append(pltpu.SemaphoreType.DMA((chunks, pens - 1)))
        scratch.append(pltpu.SemaphoreType.DMA((chunks,)))
    return pl.pallas_call(
        functools.partial(short_kernel, first, last, pens, here // ROWS),
        grid=(here // ROWS,),
        in_specs=in_specs,
        out_specs=out_specs,
        out_shape=outs,
        scratch_shapes=scratch,
        compiler_params=pltpu.CompilerParams(vmem_limit_bytes=VMEM)
        if last
        else pltpu.CompilerParams(
            vmem_limit_bytes=VMEM, collective_id=1 if first else 4, has_side_effects=True
        ),
        name="short_first" if first else "short_last" if last else "short_mid",
    )(*ins)


def long_kernel(groups, pens, wave_ref, table_ref, cos_ref, sin_ref, out_ref):
    table = table_ref[...]
    tile = 2 * LANES
    rows = out_ref.shape[4]

    def columns(q, carry):
        at = pl.ds(pl.multiple_of(q * tile, tile), tile)
        coeff = [
            jnp.dot(
                table,
                wave_ref[:, 0, c, :, at].reshape(NL, tile),
                preferred_element_type=jnp.float32,
            )
            for c in range(2)
        ]
        cosine = jnp.concatenate([cos_ref[...]] * 2, axis=1)
        sine = jnp.concatenate([sin_ref[...]] * 2, axis=1)
        turned = rotate(coeff[0], coeff[1], cosine, sine)
        for c in range(2):
            done = jnp.dot(table, turned[c].astype(jnp.bfloat16), preferred_element_type=jnp.float32)
            done = done.astype(jnp.bfloat16).reshape(pens, groups, rows, tile)
            for g in range(groups):
                out_ref[g, :, 0, c, :, at] = done[:, g]
        return carry

    lax.fori_loop(0, NS // tile, columns, 0)


def long_pass(groups, wave, table, cosine, sine):
    pens, angles, _, here, _ = wave.shape
    rows = here // groups
    return pl.pallas_call(
        functools.partial(long_kernel, groups, pens),
        grid=(angles,),
        in_specs=[
            pl.BlockSpec((pens, 1, 2, here, NS), lambda i: (0, i, 0, 0, 0)),
            pl.BlockSpec((NL, NL), lambda i: (0, 0)),
            pl.BlockSpec((NL, LANES), lambda i: (0, 0)),
            pl.BlockSpec((NL, LANES), lambda i: (0, 0)),
        ],
        out_specs=pl.BlockSpec((groups, pens, 1, 2, rows, NS), lambda i: (0, 0, i, 0, 0, 0)),
        out_shape=jax.ShapeDtypeStruct((groups, pens, angles, 2, rows, NS), jnp.bfloat16),
        compiler_params=pltpu.CompilerParams(vmem_limit_bytes=VMEM),
        name="long_pass",
    )(wave, table, cosine, sine)


def angle_kernel(wave_ref, table_ref, table_t_ref, inv_long_ref, inv_short_ref, rotor_ref, out_ref, stage, blocks, send_sem, recv_sem, local_sem):
    rows = out_ref.shape[1]
    groups, share = out_ref.shape[0], out_ref.shape[3]
    pitch = 2 * rows + PAD
    for a in range(NANG):
        for c in range(2):
            stage[a * pitch + c * rows : a * pitch + (c + 1) * rows, :] = wave_ref[a, c].astype(jnp.float32)
    rotor = rotor_ref[...]
    chunk = pl.program_id(0)
    g, p = lax.axis_index("grp"), lax.axis_index("pen")
    spots = [lax.rem(g + d, groups) for d in range(1, groups)]
    targets = [(spot, p) for spot in spots]

    @pl.when(chunk == 0)
    def _():
        greet(targets)

    def one(r):
        both = jnp.concatenate(
            [stage[pl.ds(c * rows + r, NANG, stride=pitch), :] for c in range(2)], axis=1
        ).astype(jnp.bfloat16)
        coeff = jnp.dot(table_ref[...], both, preferred_element_type=jnp.float32)
        moment = inv_long_ref[pl.ds(r, 1), :] + inv_short_ref[...]
        cosine, sine = wide_turn(time_step * jnp.minimum(rotor * moment, energy_cap))
        real, imag = rotate(coeff[:, :LANES], coeff[:, LANES:], cosine, sine)
        both = jnp.concatenate([real, imag], axis=1).astype(jnp.bfloat16)
        done = jnp.dot(table_t_ref[...], both, preferred_element_type=jnp.float32).astype(jnp.bfloat16)
        for to in range(groups):
            for c in range(2):
                blocks[chunk, to, r, c] = done[
                    to * share : (to + 1) * share, c * LANES : (c + 1) * LANES
                ]

    def four(k, carry):
        for m in range(4):
            one(k * 4 + m)
        return carry

    lax.fori_loop(0, rows // 4, four, 0)

    def source(part, spot):
        return blocks.at[part, spot]

    def landing(part, spot):
        start = part * LANES if isinstance(part, int) else pl.multiple_of(part * LANES, LANES)
        return out_ref.at[spot, :, :, :, pl.ds(start, LANES)]

    send_chunk(
        chunk, NS // LANES, g, source, landing, targets, spots, send_sem, recv_sem, local_sem
    )


def angle_pass(groups, wave, table, table_t, inv_long, inv_short, rotor):
    rows = wave.shape[2]
    share = NANG // groups
    return pl.pallas_call(
        angle_kernel,
        grid=(NS // LANES,),
        in_specs=[
            pl.BlockSpec((NANG, 2, rows, LANES), lambda i: (0, 0, 0, i)),
            pl.BlockSpec((NANG, NANG), lambda i: (0, 0)),
            pl.BlockSpec((NANG, NANG), lambda i: (0, 0)),
            pl.BlockSpec((rows, LANES), lambda i: (0, 0)),
            pl.BlockSpec((1, LANES), lambda i: (0, i)),
            pl.BlockSpec((NANG, LANES), lambda i: (0, 0)),
        ],
        out_specs=pl.BlockSpec(memory_space=pl.ANY),
        out_shape=jax.ShapeDtypeStruct((groups, rows, 2, share, NS), jnp.bfloat16),
        scratch_shapes=[pltpu.VMEM((NANG * (2 * rows + PAD), LANES), jnp.float32),
            pltpu.VMEM((NS // LANES, groups, rows, 2, share, LANES), jnp.bfloat16),
            pltpu.SemaphoreType.DMA((NS // LANES, groups - 1)),
            pltpu.SemaphoreType.DMA((NS // LANES, groups - 1)),
            pltpu.SemaphoreType.DMA((NS // LANES,)),
        ],
        compiler_params=pltpu.CompilerParams(
            vmem_limit_bytes=VMEM, collective_id=3, has_side_effects=True
        ),
        name="angle_pass",
    )(wave, table, table_t, inv_long, inv_short, rotor)


def exchange_kernel(groups, pens, x_ref, o_ref, send_sem, recv_sem, local_sem):
    g, p = lax.axis_index("grp"), lax.axis_index("pen")
    wide_g, wide_p = groups > 1, pens > 1
    count_g, count_p = lax.axis_size("grp"), lax.axis_size("pen")
    partners = [(dg, dp) for dg in range(groups) for dp in range(pens) if (dg, dp) != (0, 0)]
    partners.sort(key=lambda q: -((q[0] != 0) + (q[1] != 0)))

    def place(gg, pp):
        return (gg * pens if wide_g else 0) + (pp if wide_p else 0)

    def target(q):
        return lax.rem(g + q[0], count_g), lax.rem(p + q[1], count_p)

    barrier = pltpu.get_barrier_semaphore()
    for q in partners:
        pl.semaphore_signal(barrier, inc=1, device_id=target(q), device_id_type=MESH)
    pl.semaphore_wait(barrier, len(partners))
    me = place(g, p)
    copies = []
    for k, q in enumerate(partners):
        to = target(q)
        copy = pltpu.make_async_remote_copy(
            src_ref=x_ref.at[place(*to)],
            dst_ref=o_ref.at[me],
            send_sem=send_sem.at[k],
            recv_sem=recv_sem.at[k],
            device_id=to,
            device_id_type=MESH,
        )
        copy.start()
        copies.append(copy)
    local = pltpu.make_async_copy(x_ref.at[me], o_ref.at[me], local_sem)
    local.start()
    local.wait()
    for copy in copies:
        copy.wait()


def exchange(x, groups, pens, collective_id):
    count = groups * pens
    return pl.pallas_call(
        functools.partial(exchange_kernel, groups, pens),
        out_shape=jax.ShapeDtypeStruct(x.shape, x.dtype),
        in_specs=[pl.BlockSpec(memory_space=pl.ANY)],
        out_specs=pl.BlockSpec(memory_space=pl.ANY),
        scratch_shapes=[
            pltpu.SemaphoreType.DMA((count - 1,)),
            pltpu.SemaphoreType.DMA((count - 1,)),
            pltpu.SemaphoreType.DMA,
        ],
        compiler_params=pltpu.CompilerParams(collective_id=collective_id, has_side_effects=True),
        name="exchange_%d" % collective_id,
    )(x)


def route_matrix(route_owner, route_row, route_weight, pens):
    lines = route_owner.shape[2]
    keys = (route_owner * PSROWS + route_row).reshape(lines, 2)
    weights = route_weight.reshape(lines, 2)
    targets = jnp.arange(pens * PSROWS, dtype=jnp.int32)[:, None]
    total = jnp.zeros((pens * PSROWS, lines), jnp.float32)
    for k in range(2):
        total = total + jnp.where(targets == keys[None, :, k], weights[None, :, k], 0.0)
    return total.astype(jnp.bfloat16)


def on_device_tiled(
    psi, potential, absorber_region, absorber_strength, route_owner, route_row, route_weight
):
    groups, pens = lax.axis_size("grp"), lax.axis_size("pen")
    here, angles = potential.shape[:2]
    rows = here // groups
    share = NANG // (groups * pens)
    table_short = jnp.asarray(sine_constant(NS))
    table_long = jnp.asarray(sine_constant(NL))
    angular_np = legendre_constant(NANG)
    angular, angular_t = jnp.asarray(angular_np), jnp.asarray(angular_np.T)
    short_phase = jnp.asarray(phase_constant(NS))
    long_phase = phase_constant(NL)
    long_cos = jnp.broadcast_to(jnp.asarray(long_phase[0])[:, None], (NL, LANES))
    long_sin = jnp.broadcast_to(jnp.asarray(long_phase[1])[:, None], (NL, LANES))
    order = jnp.arange(NANG, dtype=jnp.float32)
    rotor = jnp.broadcast_to((order * (order + 1.0))[:, None], (NANG, LANES))
    first_row = lax.axis_index("pen") * here + lax.axis_index("grp") * rows
    inv_long = inverse_moment(first_row + jnp.arange(rows, dtype=jnp.int32))
    inv_long = jnp.broadcast_to(inv_long[:, None], (rows, LANES))
    inv_short = inverse_moment(jnp.arange(NS, dtype=jnp.int32))[None, :]
    keep = absorber_keep(absorber_region, absorber_strength)
    routes = route_matrix(route_owner, route_row, route_weight, pens)

    flux = jnp.zeros((pens * PSROWS, 2 * RABS), jnp.float32)
    (wave,) = short_pass(True, False, pens, psi, potential, keep, table_short, short_phase)
    for step in range(STEPS):
        wave = long_pass(groups, wave, table_long, long_cos, long_sin)
        wave = exchange(wave.reshape(groups * pens, share, 2, rows, NS), groups, pens, 2)
        wave = angle_pass(
            groups, wave.reshape(NANG, 2, rows, NS), angular, angular_t, inv_long, inv_short, rotor
        )
        wave = wave.reshape(here, 2, angles, NS)
        if step + 1 < STEPS:
            lost, wave = short_pass(False, False, pens, wave, potential, keep, table_short, short_phase)
        else:
            state, lost = short_pass(False, True, pens, wave, potential, keep, table_short, short_phase)
        flux = flux + jnp.dot(
            routes, lost.reshape(here * angles, 2 * RABS), preferred_element_type=jnp.float32
        )
    parts = lax.all_to_all(flux.reshape(pens, PSROWS, 2 * RABS), "pen", 0, 0, tiled=True)
    return (state, jnp.sum(parts, axis=0).reshape(1, 1, PSROWS, 2 * RABS))


def solution(mesh):
    groups, pens = mesh.shape["grp"], mesh.shape["pen"]
    body = on_device_tiled if tiles_fit(groups, pens) else on_device
    return jax.shard_map(
        body,
        mesh=mesh,
        in_specs=(
            P(None, "pen", "grp", None),
            P("pen", "grp", None),
            P("pen", "grp"),
            P(),
            P("grp", "pen", None, None),
            P("grp", "pen", None, None),
            P("grp", "pen", None, None),
        ),
        out_specs=(P(None, "pen", "grp", None), P("grp", "pen", None, None)),
        check_vma=False,
    )
```
